256 devices in a mesh: seq: 16 (over z_hi, x), dp: 16 (over y, z_lo, core).
Axes of the slice: x: 4, y: 4, z: 8 (z_hi: 4, z_lo: 2; z = z_hi * 2 + z_lo), core: 2. Of those that a mesh axis runs over, the one named last changes fastest.
Arguments:
- query_in: bfloat16 [16, 2048, 3072], P('dp', 'seq'), may hold values from -5 to 5
- key_in: bfloat16 [16, 2048, 3072], P('dp', 'seq'), may hold values from -5 to 5
- value_in: bfloat16 [16, 2048, 3072], P('dp', 'seq'), may hold values from -6 to 6
- cotangent: bfloat16 [16, 2048, 3072], P('dp', 'seq'), may hold values from -6 to 6
- query_bias: float32 [3072], replicated, may hold values from -3 to 3
- value_bias: float32 [3072], replicated, may hold values from -3 to 3
Outputs:
- attended: bfloat16 [16, 2048, 3072], P('dp', 'seq')
- query_grad: bfloat16 [16, 2048, 3072], P('dp', 'seq')
- key_grad: bfloat16 [16, 2048, 3072], P('dp', 'seq')
- value_grad: bfloat16 [16, 2048, 3072], P('dp', 'seq')
- query_bias_grad: float32 [3072], replicated
- value_bias_grad: float32 [3072], replicated
The draws below stay inside these ranges and needn't reach their ends.
All inputs are finite; a program needn't handle non-finite values.
Results may differ from the reference program's by a relative error of at most 0.04.
Values may be sent and summed in bfloat16 or wider, within the bound.
No kernel may reach another device: no remote copies, remote signals or barrier semaphores. Data moves between devices by JAX's collectives and lax.ppermute only.
A program may use at most 64 MiB of HBM per device.

```python
import math
import jax
import jax.numpy as jnp
from jax import lax

HD = 96
H = 32
HW = 3072
SEQ_LEN = 2048
DOCS = 16


def draw_query_in(key, part):
    key = jax.random.fold_in(key, 11)
    shape = (DOCS, SEQ_LEN, H * HD)
    base = jnp.clip(jax.random.normal(key, shape, jnp.float32), -5.0, 5.0)
    return base.astype(jnp.bfloat16)


def draw_key_in(key, part):
    key = jax.random.fold_in(key, 23)
    shape = (DOCS, SEQ_LEN, H * HD)
    base = jnp.clip(jax.random.normal(key, shape, jnp.float32), -5.0, 5.0)
    return base.astype(jnp.bfloat16)


def levels(rng, extent, shards, least, top_value):
    def one(dim, blocks):
        heights = jax.random.uniform(jax.random.fold_in(jax.random.fold_in(rng, 6), dim), (blocks,), jnp.float32, least / len(shards), top_value / len(shards))
        return jnp.repeat(jnp.exp(heights), extent[dim] // blocks).reshape((-1,) + (1,) * (len(extent) - dim - 1))

    factor_of = one(*shards[0])
    for cut in shards[1:]:
        factor_of = factor_of * one(*cut)
    return factor_of


def noise(own_key, dims, scale, reach, cuts=(), kind=jnp.bfloat16):
    values = scale * jax.random.normal(own_key, dims, jnp.float32)
    if cuts:
        values = values * levels(own_key, dims, cuts, -0.22, 0.18)
    return jnp.clip(values, -reach, reach).astype(kind)


def setup_inputs(seed: int = 0) -> dict:
    streams_of = jax.random.split(jax.random.key(seed), 7)
    return {
        "query_in": draw_query_in(jax.random.fold_in(streams_of[6], 71), 0),
        "key_in": draw_key_in(jax.random.fold_in(streams_of[6], 71), 0),
        "value_in": noise(streams_of[2], (DOCS, SEQ_LEN, HW), 1.0, 6.0, ((0, 16), (1, 16))),
        "cotangent": noise(streams_of[3], (DOCS, SEQ_LEN, HW), 1.0, 6.0, ((0, 16), (1, 16))),
        "query_bias": noise(streams_of[4], (HW,), 0.5, 3.0, (), jnp.float32),
        "value_bias": noise(streams_of[5], (HW,), 0.5, 3.0, (), jnp.float32),
    }


def attend(query, keys, values, cotan):
    length, heads, width = query.shape
    scale = 1.0 / math.sqrt(width)
    block = min(512, length)
    count = length // block
    key_pos = jnp.arange(length)
    query_f = query.astype(jnp.float32)
    keys_f = keys.astype(jnp.float32)
    values_f = values.astype(jnp.float32)
    cotan_f = cotan.astype(jnp.float32)

    def step(carry, index):
        dk_acc, dv_acc = carry
        start = (index * block).astype(jnp.int32)
        q_blk = lax.dynamic_slice_in_dim(query_f, start, block, 0)
        g_blk = lax.dynamic_slice_in_dim(cotan_f, start, block, 0)
        scores = jnp.einsum('qhd,khd->hqk', q_blk, keys_f) * scale
        q_pos = start + jnp.arange(block)
        allowed = key_pos[None, :] <= q_pos[:, None]
        scores = jnp.where(allowed[None], scores, -1e+30)
        top = lax.optimization_barrier(jnp.max(scores, axis=-1, keepdims=True))
        expo = jnp.exp(scores - top)
        probs = expo / lax.optimization_barrier(jnp.sum(expo, axis=-1, keepdims=True))
        weights = probs.astype(jnp.bfloat16).astype(jnp.float32)
        out = jnp.einsum('hqk,khd->qhd', weights, values_f).astype(jnp.bfloat16)
        dv_acc = dv_acc + jnp.einsum('hqk,qhd->khd', weights, g_blk)
        dprobs = jnp.einsum('qhd,khd->hqk', g_blk, values_f)
        delta = lax.optimization_barrier(jnp.sum(g_blk * out.astype(jnp.float32), axis=-1))
        dscores = (probs * (dprobs - jnp.transpose(delta)[:, :, None])).astype(jnp.bfloat16).astype(jnp.float32)
        d_query = (jnp.einsum('hqk,khd->qhd', dscores, keys_f) * scale).astype(jnp.bfloat16)
        dk_acc = dk_acc + jnp.einsum('hqk,qhd->khd', dscores, q_blk) * scale
        return ((dk_acc, dv_acc), (out, d_query))
    zeros = jnp.zeros((length, heads, width), jnp.float32)
    (dk_sum, dv_sum), (outs, dqs) = lax.scan(step, (zeros, zeros), jnp.arange(count))
    outs = outs.reshape(length, heads, width)
    dqs = dqs.reshape(length, heads, width)
    return (outs, dqs, dk_sum.astype(jnp.bfloat16), dv_sum.astype(jnp.bfloat16))

def reference(query_in, key_in, value_in, cotangent, query_bias, value_bias):
    queries = (query_in.astype(jnp.float32) + query_bias).astype(jnp.bfloat16)
    values = (value_in.astype(jnp.float32) + value_bias).astype(jnp.bfloat16)

    def per_doc(items):
        shaped = [item.reshape(SEQ_LEN, H, HD) for item in items]
        results = attend(shaped[0], shaped[1], shaped[2], shaped[3])
        return tuple((r.reshape(SEQ_LEN, H * HD) for r in results))
    attended, query_grad, key_grad, value_grad = lax.map(per_doc, (queries, key_in, values, cotangent))
    factor = 8.0 / math.sqrt(SEQ_LEN * DOCS)
    query_bias_grad = lax.optimization_barrier(jnp.sum(query_grad.astype(jnp.float32), axis=(0, 1))) * factor
    value_bias_grad = lax.optimization_barrier(jnp.sum(value_grad.astype(jnp.float32), axis=(0, 1))) * factor
    return (attended, query_grad, key_grad, value_grad, query_bias_grad, value_bias_grad)
```

```python
import functools
import math

import jax
import jax.numpy as jnp
from jax import lax
from jax.experimental import pallas as pl
from jax.experimental.pallas import tpu as pltpu
from jax.sharding import PartitionSpec as P

HD = 96
H = 32
PAD = 128
F32 = jnp.float32
BF16 = jnp.bfloat16
SCALE = 1.0 / math.sqrt(HD)
TILE = 512


def dot(a, b):
    return jnp.dot(a, b, preferred_element_type=F32)


def pack_kernel(q_ref, k_ref, v_ref, g_ref, qb_ref, vb_ref, out_ref):
    heads = out_ref.shape[0]
    tensors = (
        (q_ref[...].astype(F32) + qb_ref[...]).astype(BF16).astype(F32),
        k_ref[...].astype(F32),
        (v_ref[...].astype(F32) + vb_ref[...]).astype(BF16).astype(F32),
        g_ref[...].astype(F32),
    )
    for t, x in enumerate(tensors):
        turned = x.T.astype(BF16)
        for h in range(heads):
            out_ref[h, t * HD : (t + 1) * HD, :] = turned[h * HD : (h + 1) * HD, :]


def pack(arrays, query_bias, value_bias, chunk, groups):
    rows, width = arrays[0].shape
    heads = 4
    block = heads * HD
    steps = groups // heads
    first = chunk * steps
    data = pl.BlockSpec((rows, block), lambda i: (0, first + i))
    bias = pl.BlockSpec((1, block), lambda i: (0, first + i))
    return pl.pallas_call(
        pack_kernel,
        grid=(steps,),
        in_specs=[data] * 4 + [bias] * 2,
        out_specs=pl.BlockSpec((heads, 4 * HD, rows), lambda i: (i, 0, 0)),
        out_shape=jax.ShapeDtypeStruct((groups, 4 * HD, rows), BF16),
        compiler_params=pltpu.CompilerParams(vmem_limit_bytes=32 << 20),
        cost_estimate=pl.CostEstimate(flops=0, bytes_accessed=8 * rows * steps * block * 2, transcendentals=0),
        name="pack",
    )(*arrays, query_bias, value_bias)


def unpack_kernel(in_ref, *refs):
    outs = refs[-4:]
    heads = in_ref.shape[0]
    for t, out_ref in enumerate(outs):
        x = jnp.concatenate([in_ref[h, t * HD : (t + 1) * HD, :].astype(F32) for h in range(heads)], axis=0)
        out_ref[...] = x.T.astype(BF16)


def unpack(back, chunk, width, held):
    groups, _, rows = back.shape
    heads = 4
    block = heads * HD
    steps = groups // heads
    first = chunk * steps
    shape = jax.ShapeDtypeStruct((rows, width), BF16)
    return pl.pallas_call(
        unpack_kernel,
        grid=(steps,),
        in_specs=[pl.BlockSpec((heads, 4 * HD, rows), lambda i: (i, 0, 0))]
        + [pl.BlockSpec(memory_space=pl.ANY)] * len(held),
        out_specs=[pl.BlockSpec((rows, block), lambda i: (0, first + i))] * 4,
        out_shape=[shape] * 4,
        input_output_aliases={1 + t: t for t in range(len(held))},
        compiler_params=pltpu.CompilerParams(vmem_limit_bytes=32 << 20),
        cost_estimate=pl.CostEstimate(flops=0, bytes_accessed=8 * rows * steps * block * 2, transcendentals=0),
        name="unpack",
    )(back, *held)


def attend_kernel(
    chunk, in_ref, out_ref, bias_ref, qt, kt, vt, gt, qn, kn, vn, gn, s_buf, dp_buf, ot, dqt, dk, dv
):
    blocks, _, rows = in_ref.shape
    length = blocks * rows
    tiles = length // TILE
    per = TILE // rows
    base2 = SCALE * math.log2(math.e)

    spare = jnp.zeros((PAD - HD, rows), BF16)
    for b in range(blocks):
        for t, (turned, plain) in enumerate(((qt, qn), (kt, kn), (vt, vn), (gt, gn))):
            block = jnp.concatenate([in_ref[b, t * HD : (t + 1) * HD, :], spare], axis=0)
            turned[:, b * rows : (b + 1) * rows] = block
            plain[b * rows : (b + 1) * rows, :] = block.astype(F32).T.astype(BF16)
    dk[...] = jnp.zeros_like(dk)
    dv[...] = jnp.zeros_like(dv)

    visible = lax.broadcasted_iota(jnp.int32, (TILE, TILE), 0) <= lax.broadcasted_iota(
        jnp.int32, (TILE, TILE), 1
    )
    sum_q = jnp.zeros((PAD, rows), F32)

    for i in range(tiles):
        cols = slice(i * TILE, (i + 1) * TILE)
        qt_i, gt_i = qt[:, cols], gt[:, cols]
        qn_i, gn_i = qn[cols, :], gn[cols, :]

        def score(j, top, diagonal):
            at = pl.ds(pl.multiple_of(j * TILE, TILE), TILE)
            s = dot(kn[at, :], qt_i)
            if diagonal:
                s = jnp.where(visible, s, -1e30)
            s_buf[at, :] = s
            dp_buf[at, :] = dot(vn[at, :], gt_i)
            return jnp.maximum(top, jnp.max(s, axis=0, keepdims=True))

        top = jnp.full((1, TILE), -1e30, F32)
        top = lax.fori_loop(0, i, lambda j, c: score(j, c, False), top)
        top = score(i, top, True) * base2

        def expo(j, carry):
            total, delta = carry
            at = pl.ds(pl.multiple_of(j * TILE, TILE), TILE)
            p = jnp.exp2(s_buf[at, :] * base2 - top)
            s_buf[at, :] = p
            total = total + jnp.sum(p, axis=0, keepdims=True)
            delta = delta + jnp.sum(p * dp_buf[at, :], axis=0, keepdims=True)
            return total, delta

        zero = jnp.zeros((1, TILE), F32)
        total, delta = lax.fori_loop(0, i + 1, expo, (zero, zero))
        inverse = 1.0 / total
        delta = delta * inverse

        ot[...] = jnp.zeros_like(ot)
        dqt[...] = jnp.zeros_like(dqt)

        def grads(j, carry):
            at = pl.ds(pl.multiple_of(j * TILE, TILE), TILE)
            probs = s_buf[at, :] * inverse
            weights = probs.astype(BF16)
            dscores = (probs * (dp_buf[at, :] - delta)).astype(BF16)
            ot[...] += dot(vt[:, at], weights)
            dqt[...] += dot(kt[:, at], dscores)
            dv[at, :] += dot(weights, gn_i)
            dk[at, :] += dot(dscores, qn_i)
            return carry

        lax.fori_loop(0, i + 1, grads, 0)
        for b in range(per):
            part = slice(b * rows, (b + 1) * rows)
            out_ref[i * per + b, 0:HD, :] = ot[:HD, part].astype(BF16)
            dq = (dqt[:, part] * SCALE).astype(BF16)
            out_ref[i * per + b, HD : 2 * HD, :] = dq[:HD, :]
            sum_q = sum_q + dq.astype(F32)

    sum_v = jnp.zeros((rows, PAD), F32)
    for b in range(blocks):
        part = slice(b * rows, (b + 1) * rows)
        out_ref[b, 2 * HD : 3 * HD, :] = (dk[part, :] * SCALE).T.astype(BF16)[:HD, :]
        dvb = dv[part, :].astype(BF16).astype(F32)
        out_ref[b, 3 * HD : 4 * HD, :] = dvb.T.astype(BF16)[:HD, :]
        sum_v = sum_v + dvb
    row = lax.broadcasted_iota(jnp.int32, bias_ref.shape, 0)
    sums_q = jnp.sum(sum_q.T, axis=0, keepdims=True)
    sums_v = jnp.sum(sum_v, axis=0, keepdims=True)
    bias_ref[...] = jnp.where(
        row == 2 * chunk, sums_q, jnp.where(row == 2 * chunk + 1, sums_v, 0.0)
    )


def attend(pieces, chunk):
    blocks, _, rows = pieces.shape
    length = blocks * rows
    flops = 6 * length * length * PAD
    return pl.pallas_call(
        functools.partial(attend_kernel, chunk),
        in_specs=[pl.BlockSpec(memory_space=pltpu.VMEM)],
        out_specs=[pl.BlockSpec(memory_space=pltpu.VMEM)] * 2,
        out_shape=[
            jax.ShapeDtypeStruct(pieces.shape, BF16),
            jax.ShapeDtypeStruct((8, PAD), F32),
        ],
        scratch_shapes=[pltpu.VMEM((PAD, length), BF16)] * 4
        + [pltpu.VMEM((length, PAD), BF16)] * 4
        + [pltpu.VMEM((length, TILE), F32)] * 2
        + [pltpu.VMEM((PAD, TILE), F32)] * 2
        + [pltpu.VMEM((length, PAD), F32)] * 2,
        compiler_params=pltpu.CompilerParams(vmem_limit_bytes=40 << 20),
        cost_estimate=pl.CostEstimate(
            flops=flops, bytes_accessed=4 * pieces.size, transcendentals=length * length // 2
        ),
        name="attend",
    )(pieces)


def body(query_in, key_in, value_in, cotangent, query_bias, value_bias):
    groups = lax.axis_size("seq")
    parts = lax.axis_size("dp")
    docs, rows, width = query_in.shape
    chunks = H // groups
    factor = 8.0 / math.sqrt(rows * groups * docs * parts)
    arrays = [x.reshape(rows, width) for x in (query_in, key_in, value_in, cotangent)]
    qb, vb = query_bias.reshape(1, width), value_bias.reshape(1, width)

    def exchange(x, axis="seq"):
        return lax.all_to_all(x, axis, split_axis=0, concat_axis=0, tiled=True)

    sent = [exchange(pack(arrays, qb, vb, c, groups)) for c in range(chunks)]
    worked = [attend(sent[c], c) for c in range(chunks)]
    back = [exchange(w[0]) for w in worked]
    outs = ()
    for c in range(chunks):
        outs = unpack(back[c], c, width, outs)

    sums = sum(w[1] for w in worked)
    over_dp = exchange(jnp.broadcast_to(sums, (parts, *sums.shape)), "dp")
    total = jnp.sum(over_dp, axis=0) * factor
    heads = exchange(jnp.broadcast_to(total, (groups, *total.shape)))
    bias_grads = [
        jnp.transpose(heads[:, kind : 2 * chunks : 2, :HD], (1, 0, 2)).reshape(width) for kind in (0, 1)
    ]
    return (*[x.reshape(docs, rows, width) for x in outs], *bias_grads)


def solution(mesh):
    placed = P("dp", "seq", None)
    return jax.shard_map(
        body,
        mesh=mesh,
        in_specs=(placed, placed, placed, placed, P(), P()),
        out_specs=(placed, placed, placed, placed, P(), P()),
        check_vma=False,
    )
```

```python
import functools
import math

import jax
import jax.numpy as jnp
from jax import lax
from jax.experimental import pallas as pl
from jax.experimental.pallas import tpu as pltpu
from jax.sharding import PartitionSpec as P

HD = 96
H = 32
PAD = 128
F32 = jnp.float32
BF16 = jnp.bfloat16
SCALE = 1.0 / math.sqrt(HD)
TILE = 512
EXTRA = 16


def dot(a, b):
    return jnp.dot(a, b, preferred_element_type=F32)


def pack_kernel(q_ref, k_ref, v_ref, g_ref, qb_ref, vb_ref, out_ref):
    heads = out_ref.shape[0]
    tensors = (
        (q_ref[...].astype(F32) + qb_ref[...]).astype(BF16).astype(F32),
        k_ref[...].astype(F32),
        (v_ref[...].astype(F32) + vb_ref[...]).astype(BF16).astype(F32),
        g_ref[...].astype(F32),
    )
    for t, x in enumerate(tensors):
        turned = x.T.astype(BF16)
        for h in range(heads):
            out_ref[h, t * HD : (t + 1) * HD, :] = turned[h * HD : (h + 1) * HD, :]


def pack(arrays, query_bias, value_bias, chunk, groups):
    rows, width = arrays[0].shape
    heads = 4
    block = heads * HD
    steps = groups // heads
    first = chunk * steps
    data = pl.BlockSpec((rows, block), lambda i: (0, first + i))
    bias = pl.BlockSpec((1, block), lambda i: (0, first + i))
    return pl.pallas_call(
        pack_kernel,
        grid=(steps,),
        in_specs=[data] * 4 + [bias] * 2,
        out_specs=pl.BlockSpec((heads, 4 * HD, rows), lambda i: (i, 0, 0)),
        out_shape=jax.ShapeDtypeStruct((groups, 4 * HD, rows), BF16),
        compiler_params=pltpu.CompilerParams(vmem_limit_bytes=60 << 20),
        cost_estimate=pl.CostEstimate(flops=0, bytes_accessed=8 * rows * steps * block * 2, transcendentals=0),
        name="pack",
    )(*arrays, query_bias, value_bias)


def stamp_kernel(sums_ref, held_ref, out_ref):
    del held_ref
    sums = sums_ref[0:4, :]
    high = sums.astype(BF16)
    rest = sums - high.astype(F32)
    middle = rest.astype(BF16)
    low = (rest - middle.astype(F32)).astype(BF16)
    parts = [x.astype(F32) for x in (high, middle, low)]
    rows = jnp.concatenate(parts + [jnp.zeros_like(sums)], axis=0).astype(BF16)
    for b in range(out_ref.shape[0]):
        out_ref[b] = rows


def stamp(sums, held):
    blocks, height, rows = held.shape
    return pl.pallas_call(
        stamp_kernel,
        grid=(1,),
        in_specs=[
            pl.BlockSpec((8, PAD), lambda i: (0, 0)),
            pl.BlockSpec(memory_space=pl.ANY),
        ],
        out_specs=pl.BlockSpec((blocks, EXTRA, rows), lambda i: (0, (height - EXTRA) // EXTRA, 0)),
        out_shape=jax.ShapeDtypeStruct(held.shape, held.dtype),
        input_output_aliases={1: 0},
        name="stamp",
    )(sums, held)


def unpack_kernel(factor, *refs):
    in_ref, outs = refs[0], refs[-4:] if factor is None else refs[-6:-2]
    heads = in_ref.shape[0]
    for t, out_ref in enumerate(outs):
        x = jnp.concatenate([in_ref[h, t * HD : (t + 1) * HD, :].astype(F32) for h in range(heads)], axis=0)
        out_ref[...] = x.T.astype(BF16)
    if factor is None:
        return
    sums = []
    for h in range(heads):
        x = in_ref[h, 4 * HD :, :].astype(F32)
        sums.append((x[0:4] + x[4:8] + x[8:12])[:, :HD])
    sums = jnp.concatenate(sums, axis=1) * factor
    for kind, out_ref in enumerate(refs[-2:]):
        out_ref[0:1, :] = sums[kind : kind + 1]
        out_ref[1:2, :] = sums[kind + 2 : kind + 3]


def unpack(back, chunk, width, held, factor=None):
    groups, height, rows = back.shape
    heads = 4
    block = heads * HD
    steps = groups // heads
    first = chunk * steps
    out_specs = [pl.BlockSpec((rows, block), lambda i: (0, first + i))] * 4
    out_shape = [jax.ShapeDtypeStruct((rows, width), BF16)] * 4
    if factor is not None:
        out_specs += [pl.BlockSpec((2, block), lambda i: (0, i))] * 2
        out_shape += [jax.ShapeDtypeStruct((2, groups * HD), F32)] * 2
    return pl.pallas_call(
        functools.partial(unpack_kernel, factor),
        grid=(steps,),
        in_specs=[pl.BlockSpec((heads, height, rows), lambda i: (i, 0, 0))]
        + [pl.BlockSpec(memory_space=pl.ANY)] * len(held),
        out_specs=out_specs,
        out_shape=out_shape,
        input_output_aliases={1 + t: t for t in range(len(held))},
        compiler_params=pltpu.CompilerParams(vmem_limit_bytes=32 << 20),
        cost_estimate=pl.CostEstimate(flops=0, bytes_accessed=8 * rows * steps * block * 2, transcendentals=0),
        name="unpack",
    )(back, *held)


def attend_kernel(
    chunk, in_ref, out_ref, bias_ref, qt, kt, vt, gt, qn, kn, vn, gn, s_buf, dp_buf, ot, dqt, dk, dv
):
    blocks, _, rows = in_ref.shape
    length = blocks * rows
    tiles = length // TILE
    per = TILE // rows
    base2 = SCALE * math.log2(math.e)

    spare = jnp.zeros((PAD - HD, rows), BF16)
    for b in range(blocks):
        for t, (turned, plain) in enumerate(((qt, qn), (kt, kn), (vt, vn), (gt, gn))):
            block = jnp.concatenate([in_ref[b, t * HD : (t + 1) * HD, :], spare], axis=0)
            turned[:, b * rows : (b + 1) * rows] = block
            plain[b * rows : (b + 1) * rows, :] = block.astype(F32).T.astype(BF16)
    dk[...] = jnp.zeros_like(dk)
    dv[...] = jnp.zeros_like(dv)

    visible = lax.broadcasted_iota(jnp.int32, (TILE, TILE), 0) <= lax.broadcasted_iota(
        jnp.int32, (TILE, TILE), 1
    )
    sum_q = jnp.zeros((PAD, rows), F32)

    for i in range(tiles):
        cols = slice(i * TILE, (i + 1) * TILE)
        qt_i, gt_i = qt[:, cols], gt[:, cols]
        qn_i, gn_i = qn[cols, :], gn[cols, :]

        def score(j, top, diagonal):
            at = pl.ds(pl.multiple_of(j * TILE, TILE), TILE)
            s = dot(kn[at, :], qt_i)
            if diagonal:
                s = jnp.where(visible, s, -1e30)
            s_buf[at, :] = s
            dp_buf[at, :] = dot(vn[at, :], gt_i)
            return jnp.maximum(top, jnp.max(s, axis=0, keepdims=True))

        top = jnp.full((1, TILE), -1e30, F32)
        top = lax.fori_loop(0, i, lambda j, c: score(j, c, False), top)
        top = score(i, top, True) * base2

        def expo(j, carry):
            total, delta = carry
            at = pl.ds(pl.multiple_of(j * TILE, TILE), TILE)
            p = jnp.exp2(s_buf[at, :] * base2 - top)
            s_buf[at, :] = p
            total = total + jnp.sum(p, axis=0, keepdims=True)
            delta = delta + jnp.sum(p * dp_buf[at, :], axis=0, keepdims=True)
            return total, delta

        zero = jnp.zeros((1, TILE), F32)
        total, delta = lax.fori_loop(0, i + 1, expo, (zero, zero))
        inverse = 1.0 / total
        delta = delta * inverse

        ot[...] = jnp.zeros_like(ot)
        dqt[...] = jnp.zeros_like(dqt)

        def grads(j, carry):
            at = pl.ds(pl.multiple_of(j * TILE, TILE), TILE)
            probs = s_buf[at, :] * inverse
            weights = probs.astype(BF16)
            dscores = (probs * (dp_buf[at, :] - delta)).astype(BF16)
            ot[...] += dot(vt[:, at], weights)
            dqt[...] += dot(kt[:, at], dscores)
            dv[at, :] += dot(weights, gn_i)
            dk[at, :] += dot(dscores, qn_i)
            return carry

        lax.fori_loop(0, i + 1, grads, 0)
        for b in range(per):
            part = slice(b * rows, (b + 1) * rows)
            out_ref[i * per + b, 0:HD, :] = ot[:HD, part].astype(BF16)
            dq = (dqt[:, part] * SCALE).astype(BF16)
            out_ref[i * per + b, HD : 2 * HD, :] = dq[:HD, :]
            sum_q = sum_q + dq.astype(F32)

    sum_v = jnp.zeros((rows, PAD), F32)
    for b in range(blocks):
        part = slice(b * rows, (b + 1) * rows)
        out_ref[b, 2 * HD : 3 * HD, :] = (dk[part, :] * SCALE).T.astype(BF16)[:HD, :]
        dvb = dv[part, :].astype(BF16).astype(F32)
        out_ref[b, 3 * HD : 4 * HD, :] = dvb.T.astype(BF16)[:HD, :]
        sum_v = sum_v + dvb
    row = lax.broadcasted_iota(jnp.int32, bias_ref.shape, 0)
    sums_q = jnp.sum(sum_q.T, axis=0, keepdims=True)
    sums_v = jnp.sum(sum_v, axis=0, keepdims=True)
    bias_ref[...] = jnp.where(
        row == 2 * chunk, sums_q, jnp.where(row == 2 * chunk + 1, sums_v, 0.0)
    )


def attend(pieces, chunk, extra):
    blocks, height, rows = pieces.shape
    length = blocks * rows
    flops = 6 * length * length * PAD
    return pl.pallas_call(
        functools.partial(attend_kernel, chunk),
        in_specs=[pl.BlockSpec(memory_space=pltpu.VMEM)],
        out_specs=[pl.BlockSpec(memory_space=pltpu.VMEM)] * 2,
        out_shape=[
            jax.ShapeDtypeStruct((blocks, height + extra, rows), BF16),
            jax.ShapeDtypeStruct((8, PAD), F32),
        ],
        scratch_shapes=[pltpu.VMEM((PAD, length), BF16)] * 4
        + [pltpu.VMEM((length, PAD), BF16)] * 4
        + [pltpu.VMEM((length, TILE), F32)] * 2
        + [pltpu.VMEM((PAD, TILE), F32)] * 2
        + [pltpu.VMEM((length, PAD), F32)] * 2,
        compiler_params=pltpu.CompilerParams(vmem_limit_bytes=40 << 20),
        cost_estimate=pl.CostEstimate(
            flops=flops, bytes_accessed=4 * pieces.size, transcendentals=length * length // 2
        ),
        name="attend",
    )(pieces)


def body(query_in, key_in, value_in, cotangent, query_bias, value_bias):
    groups = lax.axis_size("seq")
    parts = lax.axis_size("dp")
    docs, rows, width = query_in.shape
    chunks = H // groups
    factor = 8.0 / math.sqrt(rows * groups * docs * parts)
    arrays = [x.reshape(rows, width) for x in (query_in, key_in, value_in, cotangent)]
    qb, vb = query_bias.reshape(1, width), value_bias.reshape(1, width)

    def exchange(x, axis="seq"):
        return lax.all_to_all(x, axis, split_axis=0, concat_axis=0, tiled=True)

    sent = [exchange(pack(arrays, qb, vb, c, groups)) for c in range(chunks)]
    first, sums_first = attend(sent[0], 0, 0)
    second, sums_second = attend(sent[1], 1, EXTRA)

    sums = sums_first + sums_second
    for flip in (1, 4, 8, 2):
        sums = sums + lax.ppermute(sums, "dp", [(d, d ^ flip) for d in range(parts)])

    outs = unpack(exchange(first), 0, width, ())
    *outs, grad_q, grad_v = unpack(exchange(stamp(sums, second)), 1, width, outs, factor)
    shaped = [x.reshape(docs, rows, width) for x in outs]
    return (*shaped, grad_q.reshape(width), grad_v.reshape(width))


def solution(mesh):
    placed = P("dp", "seq", None)
    return jax.shard_map(
        body,
        mesh=mesh,
        in_specs=(placed, placed, placed, placed, P(), P()),
        out_specs=(placed, placed, placed, placed, P(), P()),
        check_vma=False,
    )
```

```python
import functools
import math

import jax
import jax.numpy as jnp
from jax import lax
from jax.experimental import pallas as pl
from jax.experimental.pallas import tpu as pltpu
from jax.sharding import PartitionSpec as P

HD = 96
H = 32
PAD = 128
F32 = jnp.float32
BF16 = jnp.bfloat16
SCALE = 1.0 / math.sqrt(HD)
TILE = 512
SIDE = 4


def dot(a, b):
    return jnp.dot(a, b, preferred_element_type=F32)


def pack_kernel(q_ref, k_ref, v_ref, g_ref, qb_ref, vb_ref, out_ref):
    heads = out_ref.shape[0]
    tensors = (
        (q_ref[...].astype(F32) + qb_ref[...]).astype(BF16).astype(F32),
        k_ref[...].astype(F32),
        (v_ref[...].astype(F32) + vb_ref[...]).astype(BF16).astype(F32),
        g_ref[...].astype(F32),
    )
    for t, x in enumerate(tensors):
        turned = x.T.astype(BF16)
        for h in range(heads):
            out_ref[h, t * HD : (t + 1) * HD, :] = turned[h * HD : (h + 1) * HD, :]


def pack(arrays, query_bias, value_bias, chunk, groups):
    rows, width = arrays[0].shape
    heads = 4
    block = heads * HD
    steps = groups // heads
    first = chunk * steps
    data = pl.BlockSpec((rows, block), lambda i: (0, first + i))
    bias = pl.BlockSpec((1, block), lambda i: (0, first + i))
    return pl.pallas_call(
        pack_kernel,
        grid=(steps,),
        in_specs=[data] * 4 + [bias] * 2,
        out_specs=pl.BlockSpec((heads, 4 * HD, rows), lambda i: (i, 0, 0)),
        out_shape=jax.ShapeDtypeStruct((groups, 4 * HD, rows), BF16),
        compiler_params=pltpu.CompilerParams(vmem_limit_bytes=60 << 20),
        cost_estimate=pl.CostEstimate(flops=0, bytes_accessed=8 * rows * steps * block * 2, transcendentals=0),
        name="pack",
    )(*arrays, query_bias, value_bias)


def place():
    me = lax.axis_index("seq")
    return lax.div(me, SIDE), lax.rem(me, SIDE)


def ahead(x, dx):
    return lax.rem(x + dx + SIDE, SIDE)


def pack_apart_kernel(q_ref, k_ref, v_ref, g_ref, qb_ref, vb_ref, *refs):
    outs, turned = refs[:-1], refs[-1]
    tensors = (
        (q_ref[...].astype(F32) + qb_ref[...]).astype(BF16).astype(F32),
        k_ref[...].astype(F32),
        (v_ref[...].astype(F32) + vb_ref[...]).astype(BF16).astype(F32),
        g_ref[...].astype(F32),
    )
    for t, data in enumerate(tensors):
        turned[t] = data.T.astype(BF16)
    _, x = place()
    for dx in range(SIDE):
        at = pl.ds(pl.multiple_of(ahead(x, dx) * HD, 32), HD)
        for t in range(4):
            outs[dx][0, t * HD : (t + 1) * HD, :] = turned[t, at, :]


def pack_apart(arrays, query_bias, value_bias, chunk):
    rows = arrays[0].shape[0]
    block = SIDE * HD
    data = pl.BlockSpec((rows, block), lambda i: (0, chunk * SIDE + i))
    bias = pl.BlockSpec((1, block), lambda i: (0, chunk * SIDE + i))
    return pl.pallas_call(
        pack_apart_kernel,
        grid=(SIDE,),
        in_specs=[data] * 4 + [bias] * 2,
        out_specs=[pl.BlockSpec((1, 4 * HD, rows), lambda i: (i, 0, 0))] * SIDE,
        out_shape=[jax.ShapeDtypeStruct((SIDE, 4 * HD, rows), BF16)] * SIDE,
        scratch_shapes=[pltpu.VMEM((4, block, rows), BF16)],
        compiler_params=pltpu.CompilerParams(vmem_limit_bytes=60 << 20),
        cost_estimate=pl.CostEstimate(flops=0, bytes_accessed=16 * rows * SIDE * block, transcendentals=0),
        name="pack",
    )(*arrays, query_bias, value_bias)


def unpack_kernel(factor, in_ref, *refs):
    turned, spare = refs[-2:]
    outs = refs[-6:-2] if factor is None else refs[-8:-4]
    z, x = place()
    for dx in range(SIDE):
        spot = ahead(x, -dx)
        at = pl.ds(pl.multiple_of(spot * HD, 32), HD)
        for t in range(4):
            turned[t, at, :] = in_ref[0, dx, t * HD : (t + 1) * HD, :]
        if factor is not None:
            spare[pl.ds(spot, 1)] = refs[0][pl.ds(ahead(z, -pl.program_id(0)), 1), dx]
    for t, out_ref in enumerate(outs):
        out_ref[...] = turned[t].astype(F32).T.astype(BF16)
    if factor is None:
        return
    sums = jnp.concatenate([spare[h][:, :HD] for h in range(SIDE)], axis=1) * factor
    block = SIDE * HD
    for kind, out_ref in enumerate(refs[-4:-2]):
        for c in range(2):
            lanes = pl.ds(pl.multiple_of((c * SIDE + pl.program_id(0)) * block, PAD), block)
            out_ref[0:1, lanes] = sums[2 * c + kind : 2 * c + kind + 1]


def unpack(back, chunk, width, held, sums=None, factor=None):
    _, _, height, rows = back.shape
    block = SIDE * HD
    in_specs = [pl.BlockSpec((1, SIDE, height, rows), lambda i: (i, 0, 0, 0))]
    out_specs = [pl.BlockSpec((rows, block), lambda i: (0, chunk * SIDE + i))] * 4
    out_shape = [jax.ShapeDtypeStruct((rows, width), BF16)] * 4
    inputs = (back,)
    if factor is not None:
        inputs += (sums,)
        in_specs += [pl.BlockSpec((SIDE, SIDE, 8, PAD), lambda i: (0, 0, 0, 0))]
        out_specs += [pl.BlockSpec((1, width), lambda i: (0, 0))] * 2
        out_shape += [jax.ShapeDtypeStruct((1, width), F32)] * 2
    return pl.pallas_call(
        functools.partial(unpack_kernel, factor),
        grid=(SIDE,),
        in_specs=in_specs + [pl.BlockSpec(memory_space=pl.ANY)] * len(held),
        out_specs=out_specs,
        out_shape=out_shape,
        scratch_shapes=[pltpu.VMEM((4, block, rows), BF16), pltpu.VMEM((SIDE, 8, PAD), F32)],
        input_output_aliases={len(inputs) + t: t for t in range(len(held))},
        compiler_params=pltpu.CompilerParams(vmem_limit_bytes=32 << 20),
        cost_estimate=pl.CostEstimate(flops=0, bytes_accessed=16 * rows * SIDE * block, transcendentals=0),
        name="unpack",
    )(*inputs, *held)


def attend_kernel(chunk, in_ref, *refs):
    outs, refs = refs[:SIDE], refs[SIDE:]
    bias_ref, qt, kt, vt, gt, qn, kn, vn, gn, s_buf, dp_buf, ot, dqt, dk, dv, out_ref = refs
    blocks, length = SIDE * SIDE, qt.shape[1]
    rows = length // blocks
    tiles = length // TILE
    per = TILE // rows
    _, x = place()
    base2 = SCALE * math.log2(math.e)

    spare = jnp.zeros((PAD - HD, rows), BF16)
    for b in range(blocks):
        if len(in_ref.shape) == 4:
            z, dx = divmod(b, SIDE)
            at = pl.ds(pl.multiple_of((z * SIDE + ahead(x, -dx)) * rows, PAD), rows)
            block_ref = in_ref.at[z, dx]
        else:
            at, block_ref = slice(b * rows, (b + 1) * rows), in_ref.at[b]
        for t, (turned, plain) in enumerate(((qt, qn), (kt, kn), (vt, vn), (gt, gn))):
            block = jnp.concatenate([block_ref[t * HD : (t + 1) * HD, :], spare], axis=0)
            turned[:, at] = block
            plain[at, :] = block.astype(F32).T.astype(BF16)
    dk[...] = jnp.zeros_like(dk)
    dv[...] = jnp.zeros_like(dv)

    visible = lax.broadcasted_iota(jnp.int32, (TILE, TILE), 0) <= lax.broadcasted_iota(
        jnp.int32, (TILE, TILE), 1
    )
    sum_q = jnp.zeros((PAD, rows), F32)

    for i in range(tiles):
        cols = slice(i * TILE, (i + 1) * TILE)
        qt_i, gt_i = qt[:, cols], gt[:, cols]
        qn_i, gn_i = qn[cols, :], gn[cols, :]

        def score(j, top, diagonal):
            at = pl.ds(pl.multiple_of(j * TILE, TILE), TILE)
            s = dot(kn[at, :], qt_i)
            if diagonal:
                s = jnp.where(visible, s, -1e30)
            s_buf[at, :] = s
            dp_buf[at, :] = dot(vn[at, :], gt_i)
            return jnp.maximum(top, jnp.max(s, axis=0, keepdims=True))

        top = jnp.full((1, TILE), -1e30, F32)
        top = lax.fori_loop(0, i, lambda j, c: score(j, c, False), top)
        top = score(i, top, True) * base2

        def expo(j, carry):
            total, delta = carry
            at = pl.ds(pl.multiple_of(j * TILE, TILE), TILE)
            p = jnp.exp2(s_buf[at, :] * base2 - top)
            s_buf[at, :] = p
            total = total + jnp.sum(p, axis=0, keepdims=True)
            delta = delta + jnp.sum(p * dp_buf[at, :], axis=0, keepdims=True)
            return total, delta

        zero = jnp.zeros((1, TILE), F32)
        total, delta = lax.fori_loop(0, i + 1, expo, (zero, zero))
        inverse = 1.0 / total
        delta = delta * inverse

        ot[...] = jnp.zeros_like(ot)
        dqt[...] = jnp.zeros_like(dqt)

        def grads(j, carry):
            at = pl.ds(pl.multiple_of(j * TILE, TILE), TILE)
            probs = s_buf[at, :] * inverse
            weights = probs.astype(BF16)
            dscores = (probs * (dp_buf[at, :] - delta)).astype(BF16)
            ot[...] += dot(vt[:, at], weights)
            dqt[...] += dot(kt[:, at], dscores)
            dv[at, :] += dot(weights, gn_i)
            dk[at, :] += dot(dscores, qn_i)
            return carry

        lax.fori_loop(0, i + 1, grads, 0)
        for b in range(per):
            part = slice(b * rows, (b + 1) * rows)
            out_ref[i * per + b, 0:HD, :] = ot[:HD, part].astype(BF16)
            dq = (dqt[:, part] * SCALE).astype(BF16)
            out_ref[i * per + b, HD : 2 * HD, :] = dq[:HD, :]
            sum_q = sum_q + dq.astype(F32)

    sum_v = jnp.zeros((rows, PAD), F32)
    for b in range(blocks):
        part = slice(b * rows, (b + 1) * rows)
        out_ref[b, 2 * HD : 3 * HD, :] = (dk[part, :] * SCALE).T.astype(BF16)[:HD, :]
        dvb = dv[part, :].astype(BF16).astype(F32)
        out_ref[b, 3 * HD : 4 * HD, :] = dvb.T.astype(BF16)[:HD, :]
        sum_v = sum_v + dvb
    for z in range(SIDE):
        for dx in range(SIDE):
            outs[dx][z] = out_ref[z * SIDE + ahead(x, dx)]
    row = lax.broadcasted_iota(jnp.int32, bias_ref.shape, 0)
    sums_q = jnp.sum(sum_q.T, axis=0, keepdims=True)
    sums_v = jnp.sum(sum_v, axis=0, keepdims=True)
    bias_ref[...] = jnp.where(
        row == 2 * chunk, sums_q, jnp.where(row == 2 * chunk + 1, sums_v, 0.0)
    )


def attend(pieces, chunk):
    height, rows = pieces.shape[-2:]
    blocks = SIDE * SIDE
    length = blocks * rows
    flops = 6 * length * length * PAD
    *outs, sums = pl.pallas_call(
        functools.partial(attend_kernel, chunk),
        in_specs=[pl.BlockSpec(memory_space=pltpu.VMEM)],
        out_specs=[pl.BlockSpec(memory_space=pltpu.VMEM)] * (SIDE + 1),
        out_shape=[jax.ShapeDtypeStruct((SIDE, height, rows), BF16)] * SIDE
        + [jax.ShapeDtypeStruct((8, PAD), F32)],
        scratch_shapes=[pltpu.VMEM((PAD, length), BF16)] * 4
        + [pltpu.VMEM((length, PAD), BF16)] * 4
        + [pltpu.VMEM((length, TILE), F32)] * 2
        + [pltpu.VMEM((PAD, TILE), F32)] * 2
        + [pltpu.VMEM((length, PAD), F32)] * 2
        + [pltpu.VMEM((blocks, height, rows), BF16)],
        compiler_params=pltpu.CompilerParams(vmem_limit_bytes=40 << 20),
        cost_estimate=pl.CostEstimate(
            flops=flops, bytes_accessed=16 * length * HD, transcendentals=length * length // 2
        ),
        name="attend",
    )(pieces)
    return outs, sums


def hop(array, dz, dx):
    spots = [(z, x) for z in range(SIDE) for x in range(SIDE)]
    pairs = [(z * SIDE + x, (z + dz) % SIDE * SIDE + (x + dx) % SIDE) for z, x in spots]
    return lax.ppermute(array, "seq", pairs)


def along_x(blocks):
    got = [blocks[0]] + [None] * (SIDE - 1)
    for dx in (2, 1, 3):
        got[dx] = hop(blocks[dx], 0, dx)
    return jnp.stack(got, axis=1)


def along_z(blocks):
    columns = [[z * SIDE + x for z in range(SIDE)] for x in range(SIDE)]
    return lax.all_to_all(blocks, "seq", 0, 0, axis_index_groups=columns, tiled=True)


def body(query_in, key_in, value_in, cotangent, query_bias, value_bias):
    groups = lax.axis_size("seq")
    parts = lax.axis_size("dp")
    docs, rows, width = query_in.shape
    factor = 8.0 / math.sqrt(rows * groups * docs * parts)
    arrays = [x.reshape(rows, width) for x in (query_in, key_in, value_in, cotangent)]
    qb, vb = query_bias.reshape(1, width), value_bias.reshape(1, width)

    sent = pack(arrays, qb, vb, 0, groups)
    coming = lax.all_to_all(sent, "seq", split_axis=0, concat_axis=0, tiled=True)
    coming_next = along_z(along_x(pack_apart(arrays, qb, vb, 1)))
    first, sums_first = attend(coming, 0)
    back_first = along_z(along_x(first))
    second, sums_second = attend(coming_next, 1)
    turned = along_x(second)

    sums = sums_first + sums_second
    for flip in (1, 4, 8, 2):
        sums = sums + lax.ppermute(sums, "dp", [(d, d ^ flip) for d in range(parts)])
    turned, sums = lax.optimization_barrier((turned, sums))
    back_second = along_z(turned)
    sums = jnp.stack([sums] + [hop(sums, 0, dx) for dx in range(1, SIDE)])
    outs = list(unpack(back_first, 0, width, ()))
    sums, outs[0] = lax.optimization_barrier((sums, outs[0]))
    sums = jnp.stack([sums] + [hop(sums, dz, 0) for dz in range(1, SIDE)])

    *outs, grad_q, grad_v = unpack(back_second, 1, width, outs, sums, factor)
    shaped = [x.reshape(docs, rows, width) for x in outs]
    return (*shaped, grad_q.reshape(width), grad_v.reshape(width))


def solution(mesh):
    placed = P("dp", "seq", None)
    return jax.shard_map(
        body,
        mesh=mesh,
        in_specs=(placed, placed, placed, placed, P(), P()),
        out_specs=(placed, placed, placed, placed, P(), P()),
        check_vma=False,
    )
```

```python
import functools
import math

import jax
import jax.numpy as jnp
from jax import lax
from jax.experimental import pallas as pl
from jax.experimental.pallas import tpu as pltpu
from jax.sharding import PartitionSpec as P

HD = 96
H = 32
PAD = 128
F32 = jnp.float32
BF16 = jnp.bfloat16
SCALE = 1.0 / math.sqrt(HD)
TILE = 512
SIDE = 4


def dot(a, b):
    return jnp.dot(a, b, preferred_element_type=F32)


def pack_kernel(q_ref, k_ref, v_ref, g_ref, qb_ref, vb_ref, out_ref):
    heads = out_ref.shape[0]
    tensors = (
        (q_ref[...].astype(F32) + qb_ref[...]).astype(BF16),
        k_ref[...],
        (v_ref[...].astype(F32) + vb_ref[...]).astype(BF16),
        g_ref[...],
    )
    for t, x in enumerate(tensors):
        turned = x.T
        for h in range(heads):
            out_ref[h, t * HD : (t + 1) * HD, :] = turned[h * HD : (h + 1) * HD, :]


def pack(arrays, query_bias, value_bias, chunk, groups):
    rows, width = arrays[0].shape
    heads = 4
    block = heads * HD
    steps = groups // heads
    first = chunk * steps
    data = pl.BlockSpec((rows, block), lambda i: (0, first + i))
    bias = pl.BlockSpec((1, block), lambda i: (0, first + i))
    return pl.pallas_call(
        pack_kernel,
        grid=(steps,),
        in_specs=[data] * 4 + [bias] * 2,
        out_specs=pl.BlockSpec((heads, 4 * HD, rows), lambda i: (i, 0, 0)),
        out_shape=jax.ShapeDtypeStruct((groups, 4 * HD, rows), BF16),
        compiler_params=pltpu.CompilerParams(vmem_limit_bytes=60 << 20),
        cost_estimate=pl.CostEstimate(flops=0, bytes_accessed=8 * rows * steps * block * 2, transcendentals=0),
        name="pack",
    )(*arrays, query_bias, value_bias)


def place():
    me = lax.axis_index("seq")
    return lax.div(me, SIDE), lax.rem(me, SIDE)


def ahead(x, dx):
    return lax.rem(x + dx + SIDE, SIDE)


def pack_apart_kernel(q_ref, k_ref, v_ref, g_ref, qb_ref, vb_ref, *refs):
    outs, turned = refs[:-1], refs[-1]
    tensors = (
        (q_ref[...].astype(F32) + qb_ref[...]).astype(BF16),
        k_ref[...],
        (v_ref[...].astype(F32) + vb_ref[...]).astype(BF16),
        g_ref[...],
    )
    for t, data in enumerate(tensors):
        turned[t] = data.T
    _, x = place()
    for dx in range(SIDE):
        at = pl.ds(pl.multiple_of(ahead(x, dx) * HD, 32), HD)
        for t in range(4):
            outs[dx][0, t * HD : (t + 1) * HD, :] = turned[t, at, :]


def pack_apart(arrays, query_bias, value_bias, chunk):
    rows = arrays[0].shape[0]
    block = SIDE * HD
    data = pl.BlockSpec((rows, block), lambda i: (0, chunk * SIDE + i))
    bias = pl.BlockSpec((1, block), lambda i: (0, chunk * SIDE + i))
    return pl.pallas_call(
        pack_apart_kernel,
        grid=(SIDE,),
        in_specs=[data] * 4 + [bias] * 2,
        out_specs=[pl.BlockSpec((1, 4 * HD, rows), lambda i: (i, 0, 0))] * SIDE,
        out_shape=[jax.ShapeDtypeStruct((SIDE, 4 * HD, rows), BF16)] * SIDE,
        scratch_shapes=[pltpu.VMEM((4, block, rows), BF16)],
        compiler_params=pltpu.CompilerParams(vmem_limit_bytes=60 << 20),
        cost_estimate=pl.CostEstimate(flops=0, bytes_accessed=16 * rows * SIDE * block, transcendentals=0),
        name="pack",
    )(*arrays, query_bias, value_bias)


def unpack_kernel(factor, in_ref, *refs):
    turned, spare = refs[-2:]
    outs = refs[-6:-2] if factor is None else refs[-8:-4]
    z, x = place()
    for dx in range(SIDE):
        spot = ahead(x, -dx)
        at = pl.ds(pl.multiple_of(spot * HD, 32), HD)
        for t in range(4):
            turned[t, at, :] = in_ref[0, dx, t * HD : (t + 1) * HD, :]
        if factor is not None:
            spare[pl.ds(spot, 1)] = refs[0][pl.ds(ahead(z, -pl.program_id(0)), 1), dx]
    for t, out_ref in enumerate(outs):
        out_ref[...] = turned[t].T
    if factor is None:
        return
    sums = jnp.concatenate([spare[h][:, :HD] for h in range(SIDE)], axis=1) * factor
    block = SIDE * HD
    for kind, out_ref in enumerate(refs[-4:-2]):
        for c in range(2):
            lanes = pl.ds(pl.multiple_of((c * SIDE + pl.program_id(0)) * block, PAD), block)
            out_ref[0:1, lanes] = sums[2 * c + kind : 2 * c + kind + 1]


def unpack(back, chunk, width, held, sums=None, factor=None):
    _, _, height, rows = back.shape
    block = SIDE * HD
    in_specs = [pl.BlockSpec((1, SIDE, height, rows), lambda i: (i, 0, 0, 0))]
    out_specs = [pl.BlockSpec((rows, block), lambda i: (0, chunk * SIDE + i))] * 4
    out_shape = [jax.ShapeDtypeStruct((rows, width), BF16)] * 4
    inputs = (back,)
    if factor is not None:
        inputs += (sums,)
        in_specs += [pl.BlockSpec((SIDE, SIDE, 8, PAD), lambda i: (0, 0, 0, 0))]
        out_specs += [pl.BlockSpec((1, width), lambda i: (0, 0))] * 2
        out_shape += [jax.ShapeDtypeStruct((1, width), F32)] * 2
    return pl.pallas_call(
        functools.partial(unpack_kernel, factor),
        grid=(SIDE,),
        in_specs=in_specs + [pl.BlockSpec(memory_space=pl.ANY)] * len(held),
        out_specs=out_specs,
        out_shape=out_shape,
        scratch_shapes=[pltpu.VMEM((4, block, rows), BF16), pltpu.VMEM((SIDE, 8, PAD), F32)],
        input_output_aliases={len(inputs) + t: t for t in range(len(held))},
        compiler_params=pltpu.CompilerParams(vmem_limit_bytes=32 << 20),
        cost_estimate=pl.CostEstimate(flops=0, bytes_accessed=16 * rows * SIDE * block, transcendentals=0),
        name="unpack",
    )(*inputs, *held)


def attend_kernel(chunk, in_ref, *refs):
    outs, refs = refs[:SIDE], refs[SIDE:]
    bias_ref, qt, kt, vt, gt, qn, kn, vn, gn, s_buf, dp_buf, ot, dqt, dk, dv, out_ref = refs
    blocks, length = SIDE * SIDE, qt.shape[1]
    rows = length // blocks
    tiles = length // TILE
    per = TILE // rows
    _, x = place()
    base2 = SCALE * math.log2(math.e)

    spare = jnp.zeros((PAD - HD, rows), BF16)
    for b in range(blocks):
        if len(in_ref.shape) == 4:
            z, dx = divmod(b, SIDE)
            at = pl.ds(pl.multiple_of((z * SIDE + ahead(x, -dx)) * rows, PAD), rows)
            block_ref = in_ref.at[z, dx]
        else:
            at, block_ref = slice(b * rows, (b + 1) * rows), in_ref.at[b]
        for t, (turned, plain) in enumerate(((qt, qn), (kt, kn), (vt, vn), (gt, gn))):
            block = jnp.concatenate([block_ref[t * HD : (t + 1) * HD, :], spare], axis=0)
            turned[:, at] = block
            plain[at, :] = block.T
    dk[...] = jnp.zeros_like(dk)
    dv[...] = jnp.zeros_like(dv)

    half = TILE // 2
    visible = lax.broadcasted_iota(jnp.int32, (half, half), 0) <= lax.broadcasted_iota(
        jnp.int32, (half, half), 1
    )
    left, right, every = slice(0, half), slice(half, TILE), slice(0, TILE)
    sum_q = jnp.zeros((PAD, rows), F32)

    for i in range(tiles):
        cols = slice(i * TILE, (i + 1) * TILE)
        qt_i, gt_i = qt[:, cols], gt[:, cols]
        qn_i, gn_i = qn[cols, :], gn[cols, :]

        upper = slice(i * TILE, i * TILE + half)
        lower = slice(i * TILE + half, (i + 1) * TILE)

        def score(j, top):
            at = pl.ds(pl.multiple_of(j * TILE, TILE), TILE)
            s = dot(kn[at, :], qt_i)
            s_buf[at, :] = s
            return jnp.maximum(top, jnp.max(s, axis=0, keepdims=True))

        top = lax.fori_loop(0, i, score, jnp.full((1, TILE), -1e30, F32))
        s = dot(kn[upper, :], qt_i)
        s = jnp.concatenate([jnp.where(visible, s[:, left], -1e30), s[:, right]], axis=1)
        s_buf[upper, :] = s
        top = jnp.maximum(top, jnp.max(s, axis=0, keepdims=True))
        s = jnp.where(visible, dot(kn[lower, :], qt_i[:, right]), -1e30)
        s_buf[lower, right] = s
        top = jnp.concatenate(
            [top[:, left], jnp.maximum(top[:, right], jnp.max(s, axis=0, keepdims=True))], axis=1
        )
        top = top * base2

        def expo(at, lanes, carry):
            total, delta = carry
            dp = dot(vn[at, :], gt_i[:, lanes])
            p = jnp.exp2(s_buf[at, lanes] * base2 - top[:, lanes])
            s_buf[at, lanes] = p
            dp_buf[at, lanes] = dp
            total = total + jnp.sum(p, axis=0, keepdims=True)
            delta = delta + jnp.sum(p * dp, axis=0, keepdims=True)
            return total, delta

        def whole(j):
            return pl.ds(pl.multiple_of(j * TILE, TILE), TILE)

        sums = (jnp.zeros((1, TILE), F32), jnp.zeros((1, TILE), F32))
        sums = lax.fori_loop(0, i, lambda j, c: expo(whole(j), every, c), sums)
        sums = expo(upper, every, sums)
        ends = expo(lower, right, tuple(x[:, right] for x in sums))
        total, delta = (jnp.concatenate([x[:, left], y], axis=1) for x, y in zip(sums, ends))
        inverse = 1.0 / total
        delta = delta * inverse

        ot[...] = jnp.zeros_like(ot)
        dqt[...] = jnp.zeros_like(dqt)

        def grads(at, lanes):
            probs = s_buf[at, lanes] * inverse[:, lanes]
            weights = probs.astype(BF16)
            dscores = (probs * (dp_buf[at, lanes] - delta[:, lanes])).astype(BF16)
            ot[:, lanes] += dot(vt[:, at], weights)
            dqt[:, lanes] += dot(kt[:, at], dscores)
            dv[at, :] += dot(weights, gn_i[lanes, :])
            dk[at, :] += dot(dscores, qn_i[lanes, :])

        def grads_whole(j, carry):
            grads(whole(j), every)
            return carry

        lax.fori_loop(0, i, grads_whole, 0)
        grads(upper, every)
        grads(lower, right)
        for b in range(per):
            part = slice(b * rows, (b + 1) * rows)
            out_ref[i * per + b, 0:HD, :] = ot[:HD, part].astype(BF16)
            dq = (dqt[:, part] * SCALE).astype(BF16)
            out_ref[i * per + b, HD : 2 * HD, :] = dq[:HD, :]
            sum_q = sum_q + dq.astype(F32)

    sum_v = jnp.zeros((rows, PAD), F32)
    for b in range(blocks):
        part = slice(b * rows, (b + 1) * rows)
        out_ref[b, 2 * HD : 3 * HD, :] = (dk[part, :] * SCALE).astype(BF16).T[:HD, :]
        dvb = dv[part, :].astype(BF16)
        out_ref[b, 3 * HD : 4 * HD, :] = dvb.T[:HD, :]
        sum_v = sum_v + dvb.astype(F32)
    for z in range(SIDE):
        for dx in range(SIDE):
            outs[dx][z] = out_ref[z * SIDE + ahead(x, dx)]
    row = lax.broadcasted_iota(jnp.int32, bias_ref.shape, 0)
    sums_q = jnp.sum(sum_q.T, axis=0, keepdims=True)
    sums_v = jnp.sum(sum_v, axis=0, keepdims=True)
    bias_ref[...] = jnp.where(
        row == 2 * chunk, sums_q, jnp.where(row == 2 * chunk + 1, sums_v, 0.0)
    )


def attend(pieces, chunk):
    height, rows = pieces.shape[-2:]
    blocks = SIDE * SIDE
    length = blocks * rows
    flops = 6 * length * length * PAD
    *outs, sums = pl.pallas_call(
        functools.partial(attend_kernel, chunk),
        in_specs=[pl.BlockSpec(memory_space=pltpu.VMEM)],
        out_specs=[pl.BlockSpec(memory_space=pltpu.VMEM)] * (SIDE + 1),
        out_shape=[jax.ShapeDtypeStruct((SIDE, height, rows), BF16)] * SIDE
        + [jax.ShapeDtypeStruct((8, PAD), F32)],
        scratch_shapes=[pltpu.VMEM((PAD, length), BF16)] * 4
        + [pltpu.VMEM((length, PAD), BF16)] * 4
        + [pltpu.VMEM((length, TILE), F32)] * 2
        + [pltpu.VMEM((PAD, TILE), F32)] * 2
        + [pltpu.VMEM((length, PAD), F32)] * 2
        + [pltpu.VMEM((blocks, height, rows), BF16)],
        compiler_params=pltpu.CompilerParams(vmem_limit_bytes=40 << 20),
        cost_estimate=pl.CostEstimate(
            flops=flops, bytes_accessed=16 * length * HD, transcendentals=length * length // 2
        ),
        name="attend",
    )(pieces)
    return outs, sums


def hop(array, dz, dx):
    spots = [(z, x) for z in range(SIDE) for x in range(SIDE)]
    pairs = [(z * SIDE + x, (z + dz) % SIDE * SIDE + (x + dx) % SIDE) for z, x in spots]
    return lax.ppermute(array, "seq", pairs)


def along_x(blocks):
    got = [blocks[0]] + [None] * (SIDE - 1)
    for dx in (2, 1, 3):
        got[dx] = hop(blocks[dx], 0, dx)
    return jnp.stack(got, axis=1)


def along_z(blocks):
    columns = [[z * SIDE + x for z in range(SIDE)] for x in range(SIDE)]
    return lax.all_to_all(blocks, "seq", 0, 0, axis_index_groups=columns, tiled=True)


def body(query_in, key_in, value_in, cotangent, query_bias, value_bias):
    groups = lax.axis_size("seq")
    parts = lax.axis_size("dp")
    docs, rows, width = query_in.shape
    factor = 8.0 / math.sqrt(rows * groups * docs * parts)
    arrays = [x.reshape(rows, width) for x in (query_in, key_in, value_in, cotangent)]
    qb, vb = query_bias.reshape(1, width), value_bias.reshape(1, width)

    sent = pack(arrays, qb, vb, 0, groups)
    coming = lax.all_to_all(sent, "seq", split_axis=0, concat_axis=0, tiled=True)
    coming_next = along_z(along_x(pack_apart(arrays, qb, vb, 1)))
    first, sums_first = attend(coming, 0)
    back_first = along_z(along_x(first))
    second, sums_second = attend(coming_next, 1)
    turned = along_x(second)

    sums = sums_first + sums_second
    for flip in (1, 4, 8, 2):
        sums = sums + lax.ppermute(sums, "dp", [(d, d ^ flip) for d in range(parts)])
    turned, sums = lax.optimization_barrier((turned, sums))
    back_second = along_z(turned)
    sums = jnp.stack([sums] + [hop(sums, 0, dx) for dx in range(1, SIDE)])
    outs = list(unpack(back_first, 0, width, ()))
    sums, outs[0] = lax.optimization_barrier((sums, outs[0]))
    sums = jnp.stack([sums] + [hop(sums, dz, 0) for dz in range(1, SIDE)])

    *outs, grad_q, grad_v = unpack(back_second, 1, width, outs, sums, factor)
    shaped = [x.reshape(docs, rows, width) for x in outs]
    return (*shaped, grad_q.reshape(width), grad_v.reshape(width))


def solution(mesh):
    placed = P("dp", "seq", None)
    return jax.shard_map(
        body,
        mesh=mesh,
        in_specs=(placed, placed, placed, placed, P(), P()),
        out_specs=(placed, placed, placed, placed, P(), P()),
        check_vma=False,
    )
```

```python
import functools
import math

import jax
import jax.numpy as jnp
from jax import lax
from jax.experimental import pallas as pl
from jax.experimental.pallas import tpu as pltpu
from jax.sharding import PartitionSpec as P

HD = 96
H = 32
PAD = 128
F32 = jnp.float32
BF16 = jnp.bfloat16
SCALE = 1.0 / math.sqrt(HD)
TILE = 512
SIDE = 4


def dot(a, b):
    return jnp.dot(a, b, preferred_element_type=F32)


def pack_kernel(first, *refs):
    ins, (qb_ref, vb_ref), out_ref = refs[:4], refs[4:6], refs[6]
    came, came_sems = refs[7:]
    heads = 4
    block = heads * HD
    steps = came.shape[2] // block
    lanes = slice(first * block, (first + steps) * block)
    coming = [pltpu.make_async_copy(x.at[:, lanes], came.at[t], came_sems.at[t]) for t, x in enumerate(ins)]
    for copy in coming:
        copy.start()
    for t in range(4):
        coming[t].wait()
        for i in range(steps):
            x = came[t, :, i * block : (i + 1) * block]
            if t in (0, 2):
                bias_ref = qb_ref if t == 0 else vb_ref
                x = (x.astype(F32) + bias_ref[:, (first + i) * block : (first + i + 1) * block]).astype(BF16)
            turned = x.T
            for h in range(heads):
                out_ref[i * heads + h, t * HD : (t + 1) * HD, :] = turned[h * HD : (h + 1) * HD, :]


def pack(arrays, query_bias, value_bias, chunk, groups):
    rows = arrays[0].shape[0]
    heads = 4
    block = heads * HD
    steps = groups // heads
    return pl.pallas_call(
        functools.partial(pack_kernel, chunk * steps),
        in_specs=[pl.BlockSpec(memory_space=pltpu.HBM)] * 4 + [pl.BlockSpec(memory_space=pltpu.VMEM)] * 2,
        out_specs=pl.BlockSpec(memory_space=pltpu.VMEM),
        out_shape=jax.ShapeDtypeStruct((groups, 4 * HD, rows), BF16),
        scratch_shapes=[pltpu.VMEM((4, rows, steps * block), BF16), pltpu.SemaphoreType.DMA((4,))],
        compiler_params=pltpu.CompilerParams(vmem_limit_bytes=56 << 20),
        cost_estimate=pl.CostEstimate(flops=0, bytes_accessed=8 * rows * steps * block * 2, transcendentals=0),
        name="pack",
    )(*arrays, query_bias, value_bias)


def place():
    me = lax.axis_index("seq")
    return lax.div(me, SIDE), lax.rem(me, SIDE)


def ahead(x, dx):
    return lax.rem(x + dx + SIDE, SIDE)


def pack_apart_kernel(q_ref, k_ref, v_ref, g_ref, qb_ref, vb_ref, *refs):
    outs, turned = refs[:-1], refs[-1]
    tensors = (
        (q_ref[...].astype(F32) + qb_ref[...]).astype(BF16),
        k_ref[...],
        (v_ref[...].astype(F32) + vb_ref[...]).astype(BF16),
        g_ref[...],
    )
    for t, data in enumerate(tensors):
        turned[t] = data.T
    _, x = place()
    for dx in range(SIDE):
        at = pl.ds(pl.multiple_of(ahead(x, dx) * HD, 32), HD)
        for t in range(4):
            outs[dx][0, t * HD : (t + 1) * HD, :] = turned[t, at, :]


def pack_apart(arrays, query_bias, value_bias, chunk):
    rows = arrays[0].shape[0]
    block = SIDE * HD
    data = pl.BlockSpec((rows, block), lambda i: (0, chunk * SIDE + i))
    bias = pl.BlockSpec((1, block), lambda i: (0, chunk * SIDE + i))
    return pl.pallas_call(
        pack_apart_kernel,
        grid=(SIDE,),
        in_specs=[data] * 4 + [bias] * 2,
        out_specs=[pl.BlockSpec((1, 4 * HD, rows), lambda i: (i, 0, 0))] * SIDE,
        out_shape=[jax.ShapeDtypeStruct((SIDE, 4 * HD, rows), BF16)] * SIDE,
        scratch_shapes=[pltpu.VMEM((4, block, rows), BF16)],
        compiler_params=pltpu.CompilerParams(vmem_limit_bytes=60 << 20),
        cost_estimate=pl.CostEstimate(flops=0, bytes_accessed=16 * rows * SIDE * block, transcendentals=0),
        name="pack",
    )(*arrays, query_bias, value_bias)


def unpack_kernel(factor, in_ref, *refs):
    turned, spare = refs[-2:]
    outs = refs[-6:-2] if factor is None else refs[-8:-4]
    z, x = place()
    for dx in range(SIDE):
        spot = ahead(x, -dx)
        at = pl.ds(pl.multiple_of(spot * HD, 32), HD)
        for t in range(4):
            turned[t, at, :] = in_ref[0, dx, t * HD : (t + 1) * HD, :]
        if factor is not None:
            spare[pl.ds(spot, 1)] = refs[0][pl.ds(ahead(z, -pl.program_id(0)), 1), dx]
    for t, out_ref in enumerate(outs):
        out_ref[...] = turned[t].T
    if factor is None:
        return
    sums = jnp.concatenate([spare[h][:, :HD] for h in range(SIDE)], axis=1) * factor
    block = SIDE * HD
    for kind, out_ref in enumerate(refs[-4:-2]):
        for c in range(2):
            lanes = pl.ds(pl.multiple_of((c * SIDE + pl.program_id(0)) * block, PAD), block)
            out_ref[0:1, lanes] = sums[2 * c + kind : 2 * c + kind + 1]


def unpack(back, chunk, width, held, sums=None, factor=None):
    _, _, height, rows = back.shape
    block = SIDE * HD
    in_specs = [pl.BlockSpec((1, SIDE, height, rows), lambda i: (i, 0, 0, 0))]
    out_specs = [pl.BlockSpec((rows, block), lambda i: (0, chunk * SIDE + i))] * 4
    out_shape = [jax.ShapeDtypeStruct((rows, width), BF16)] * 4
    inputs = (back,)
    if factor is not None:
        inputs += (sums,)
        in_specs += [pl.BlockSpec((SIDE, SIDE, 8, PAD), lambda i: (0, 0, 0, 0))]
        out_specs += [pl.BlockSpec((1, width), lambda i: (0, 0))] * 2
        out_shape += [jax.ShapeDtypeStruct((1, width), F32)] * 2
    return pl.pallas_call(
        functools.partial(unpack_kernel, factor),
        grid=(SIDE,),
        in_specs=in_specs + [pl.BlockSpec(memory_space=pl.ANY)] * len(held),
        out_specs=out_specs,
        out_shape=out_shape,
        scratch_shapes=[pltpu.VMEM((4, block, rows), BF16), pltpu.VMEM((SIDE, 8, PAD), F32)],
        input_output_aliases={len(inputs) + t: t for t in range(len(held))},
        compiler_params=pltpu.CompilerParams(vmem_limit_bytes=32 << 20),
        cost_estimate=pl.CostEstimate(flops=0, bytes_accessed=16 * rows * SIDE * block, transcendentals=0),
        name="unpack",
    )(*inputs, *held)


def attend_kernel(chunk, in_ref, *refs):
    outs, refs = refs[:SIDE], refs[SIDE:]
    bias_ref, qt, kt, vt, gt, qn, kn, vn, gn, s_buf, dp_buf, ot, dqt, dk, dv, out_ref = refs
    blocks, length = SIDE * SIDE, qt.shape[1]
    rows = length // blocks
    tiles = length // TILE
    per = TILE // rows
    _, x = place()
    base2 = SCALE * math.log2(math.e)

    spare = jnp.zeros((PAD - HD, rows), BF16)
    for b in range(blocks):
        if len(in_ref.shape) == 4:
            z, dx = divmod(b, SIDE)
            at = pl.ds(pl.multiple_of((z * SIDE + ahead(x, -dx)) * rows, PAD), rows)
            block_ref = in_ref.at[z, dx]
        else:
            at, block_ref = slice(b * rows, (b + 1) * rows), in_ref.at[b]
        for t, (turned, plain) in enumerate(((qt, qn), (kt, kn), (vt, vn), (gt, gn))):
            block = jnp.concatenate([block_ref[t * HD : (t + 1) * HD, :], spare], axis=0)
            turned[:, at] = block
            plain[at, :] = block.T
    dk[...] = jnp.zeros_like(dk)
    dv[...] = jnp.zeros_like(dv)

    half = TILE // 2
    visible = lax.broadcasted_iota(jnp.int32, (half, half), 0) <= lax.broadcasted_iota(
        jnp.int32, (half, half), 1
    )
    left, right, every = slice(0, half), slice(half, TILE), slice(0, TILE)
    sum_q = jnp.zeros((PAD, rows), F32)

    for i in range(tiles):
        cols = slice(i * TILE, (i + 1) * TILE)
        qt_i, gt_i = qt[:, cols], gt[:, cols]
        qn_i, gn_i = qn[cols, :], gn[cols, :]

        upper = slice(i * TILE, i * TILE + half)
        lower = slice(i * TILE + half, (i + 1) * TILE)

        def score(j, top):
            at = pl.ds(pl.multiple_of(j * TILE, TILE), TILE)
            s = dot(kn[at, :], qt_i)
            s_buf[at, :] = s
            return jnp.maximum(top, jnp.max(s, axis=0, keepdims=True))

        top = lax.fori_loop(0, i, score, jnp.full((1, TILE), -1e30, F32))
        s = dot(kn[upper, :], qt_i)
        s = jnp.concatenate([jnp.where(visible, s[:, left], -1e30), s[:, right]], axis=1)
        s_buf[upper, :] = s
        top = jnp.maximum(top, jnp.max(s, axis=0, keepdims=True))
        s = jnp.where(visible, dot(kn[lower, :], qt_i[:, right]), -1e30)
        s_buf[lower, right] = s
        top = jnp.concatenate(
            [top[:, left], jnp.maximum(top[:, right], jnp.max(s, axis=0, keepdims=True))], axis=1
        )
        top = top * base2

        def expo(at, lanes, carry):
            total, delta = carry
            dp = dot(vn[at, :], gt_i[:, lanes])
            p = jnp.exp2(s_buf[at, lanes] * base2 - top[:, lanes])
            s_buf[at, lanes] = p
            dp_buf[at, lanes] = dp
            total = total + jnp.sum(p, axis=0, keepdims=True)
            delta = delta + jnp.sum(p * dp, axis=0, keepdims=True)
            return total, delta

        def whole(j):
            return pl.ds(pl.multiple_of(j * TILE, TILE), TILE)

        sums = (jnp.zeros((1, TILE), F32), jnp.zeros((1, TILE), F32))
        sums = lax.fori_loop(0, i, lambda j, c: expo(whole(j), every, c), sums)
        sums = expo(upper, every, sums)
        ends = expo(lower, right, tuple(x[:, right] for x in sums))
        total, delta = (jnp.concatenate([x[:, left], y], axis=1) for x, y in zip(sums, ends))
        inverse = 1.0 / total
        delta = delta * inverse

        ot[...] = jnp.zeros_like(ot)
        dqt[...] = jnp.zeros_like(dqt)

        def grads(at, lanes):
            probs = s_buf[at, lanes] * inverse[:, lanes]
            weights = probs.astype(BF16)
            dscores = (probs * (dp_buf[at, lanes] - delta[:, lanes])).astype(BF16)
            ot[:, lanes] += dot(vt[:, at], weights)
            dqt[:, lanes] += dot(kt[:, at], dscores)
            dv[at, :] += dot(weights, gn_i[lanes, :])
            dk[at, :] += dot(dscores, qn_i[lanes, :])

        def grads_whole(j, carry):
            grads(whole(j), every)
            return carry

        lax.fori_loop(0, i, grads_whole, 0)
        grads(upper, every)
        grads(lower, right)
        for b in range(per):
            part = slice(b * rows, (b + 1) * rows)
            out_ref[i * per + b, 0:HD, :] = ot[:HD, part].astype(BF16)
            dq = (dqt[:, part] * SCALE).astype(BF16)
            out_ref[i * per + b, HD : 2 * HD, :] = dq[:HD, :]
            sum_q = sum_q + dq.astype(F32)

    sum_v = jnp.zeros((rows, PAD), F32)
    for b in range(blocks):
        part = slice(b * rows, (b + 1) * rows)
        out_ref[b, 2 * HD : 3 * HD, :] = (dk[part, :] * SCALE).astype(BF16).T[:HD, :]
        dvb = dv[part, :].astype(BF16)
        out_ref[b, 3 * HD : 4 * HD, :] = dvb.T[:HD, :]
        sum_v = sum_v + dvb.astype(F32)
    for z in range(SIDE):
        for dx in range(SIDE):
            outs[dx][z] = out_ref[z * SIDE + ahead(x, dx)]
    row = lax.broadcasted_iota(jnp.int32, bias_ref.shape, 0)
    sums_q = jnp.sum(sum_q.T, axis=0, keepdims=True)
    sums_v = jnp.sum(sum_v, axis=0, keepdims=True)
    bias_ref[...] = jnp.where(
        row == 2 * chunk, sums_q, jnp.where(row == 2 * chunk + 1, sums_v, 0.0)
    )


def attend(pieces, chunk):
    height, rows = pieces.shape[-2:]
    blocks = SIDE * SIDE
    length = blocks * rows
    flops = 6 * length * length * PAD
    *outs, sums = pl.pallas_call(
        functools.partial(attend_kernel, chunk),
        in_specs=[pl.BlockSpec(memory_space=pltpu.VMEM)],
        out_specs=[pl.BlockSpec(memory_space=pltpu.VMEM)] * (SIDE + 1),
        out_shape=[jax.ShapeDtypeStruct((SIDE, height, rows), BF16)] * SIDE
        + [jax.ShapeDtypeStruct((8, PAD), F32)],
        scratch_shapes=[pltpu.VMEM((PAD, length), BF16)] * 4
        + [pltpu.VMEM((length, PAD), BF16)] * 4
        + [pltpu.VMEM((length, TILE), F32)] * 2
        + [pltpu.VMEM((PAD, TILE), F32)] * 2
        + [pltpu.VMEM((length, PAD), F32)] * 2
        + [pltpu.VMEM((blocks, height, rows), BF16)],
        compiler_params=pltpu.CompilerParams(vmem_limit_bytes=40 << 20),
        cost_estimate=pl.CostEstimate(
            flops=flops, bytes_accessed=16 * length * HD, transcendentals=length * length // 2
        ),
        name="attend",
    )(pieces)
    return outs, sums


def hop(array, dz, dx):
    spots = [(z, x) for z in range(SIDE) for x in range(SIDE)]
    pairs = [(z * SIDE + x, (z + dz) % SIDE * SIDE + (x + dx) % SIDE) for z, x in spots]
    return lax.ppermute(array, "seq", pairs)


def along_x(blocks):
    got = [blocks[0]] + [None] * (SIDE - 1)
    for dx in (2, 1, 3):
        got[dx] = hop(blocks[dx], 0, dx)
    return jnp.stack(got, axis=1)


def along_z(blocks):
    columns = [[z * SIDE + x for z in range(SIDE)] for x in range(SIDE)]
    return lax.all_to_all(blocks, "seq", 0, 0, axis_index_groups=columns, tiled=True)


def body(query_in, key_in, value_in, cotangent, query_bias, value_bias):
    groups = lax.axis_size("seq")
    parts = lax.axis_size("dp")
    docs, rows, width = query_in.shape
    factor = 8.0 / math.sqrt(rows * groups * docs * parts)
    arrays = [x.reshape(rows, width) for x in (query_in, key_in, value_in, cotangent)]
    qb, vb = query_bias.reshape(1, width), value_bias.reshape(1, width)

    sent = pack(arrays, qb, vb, 0, groups)
    coming = lax.all_to_all(sent, "seq", split_axis=0, concat_axis=0, tiled=True)
    coming_next = along_z(along_x(pack_apart(arrays, qb, vb, 1)))
    first, sums_first = attend(coming, 0)
    back_first = along_z(along_x(first))
    second, sums_second = attend(coming_next, 1)
    turned = along_x(second)

    sums = sums_first + sums_second
    for flip in (1, 4, 8, 2):
        sums = sums + lax.ppermute(sums, "dp", [(d, d ^ flip) for d in range(parts)])
    turned, sums = lax.optimization_barrier((turned, sums))
    back_second = along_z(turned)
    sums = jnp.stack([sums] + [hop(sums, 0, dx) for dx in range(1, SIDE)])
    outs = list(unpack(back_first, 0, width, ()))
    sums, outs[0] = lax.optimization_barrier((sums, outs[0]))
    sums = jnp.stack([sums] + [hop(sums, dz, 0) for dz in range(1, SIDE)])

    *outs, grad_q, grad_v = unpack(back_second, 1, width, outs, sums, factor)
    shaped = [x.reshape(docs, rows, width) for x in outs]
    return (*shaped, grad_q.reshape(width), grad_v.reshape(width))


def solution(mesh):
    placed = P("dp", "seq", None)
    return jax.shard_map(
        body,
        mesh=mesh,
        in_specs=(placed, placed, placed, placed, P(), P()),
        out_specs=(placed, placed, placed, placed, P(), P()),
        check_vma=False,
    )
```
